256 devices in a mesh: row: 16 (over x, y), col: 16 (over z, core).
Axes of the slice: x: 4, y: 4, z: 8, core: 2. Of those that a mesh axis runs over, the one named last changes fastest.
Arguments:
- activations: bfloat16 [2048, 16384], P('col', 'row'), may hold values from -6 to 6
- grad_output: bfloat16 [2048, 16384], P('col', 'row'), may hold values from -6 to 6
- gate_pre: bfloat16 [2048, 8192], P('row', 'col'), may hold values from -8 to 8
- up_pre: bfloat16 [2048, 8192], P('row', 'col'), may hold values from -6 to 6
- w_gate: bfloat16 [16384, 8192], P('row', 'col'), may hold values from -0.046875 to 0.046875
- w_up: bfloat16 [16384, 8192], P('row', 'col'), may hold values from -0.046875 to 0.046875
- w_down: bfloat16 [8192, 16384], P('col', 'row'), may hold values from -0.0625 to 0.0625
Outputs:
- grad_input: bfloat16 [2048, 16384], P('col', 'row')
- grad_gate: bfloat16 [16384, 8192], P('row', 'col')
- grad_up: bfloat16 [16384, 8192], P('row', 'col')
- grad_down: bfloat16 [8192, 16384], P('col', 'row')
The draws below stay inside these ranges and needn't reach their ends.
All inputs are finite; a program needn't handle non-finite values.
Results may differ from the reference program's by a relative error of at most 0.005.
Values may be sent and summed in bfloat16 or wider, within the bound.
No kernel may reach another device: no remote copies, remote signals or barrier semaphores. Data moves between devices by JAX's collectives and lax.ppermute only.
A program may use at most 128 MiB of HBM per device.

```python
import jax
import jax.numpy as jnp
from jax import lax

D = 16384
FF = 8192
TOKENS = 2048


def block_scale(rng, dims, pieces, low, largest):
    gain = 1.0
    for axis_at, blocks in pieces:
        draws = jax.random.uniform(jax.random.fold_in(jax.random.fold_in(rng, 6), axis_at), (blocks,), jnp.float32, low / len(pieces), largest / len(pieces))
        gain = gain * jnp.repeat(jnp.exp(draws), dims[axis_at] // blocks).reshape((-1,) + (1,) * (len(dims) - 1 - axis_at))
    return gain


def normal_values(stream_key, shape, scale, reach, pieces=(), held_as=jnp.bfloat16):
    factor_of = block_scale(stream_key, shape, pieces, -0.22, 0.18) if pieces else 1.0
    values = jax.random.normal(stream_key, shape, jnp.float32) * scale * factor_of
    return jnp.minimum(jnp.maximum(values, -reach), reach).astype(held_as)


def setup_inputs(seed: int = 0) -> dict:
    splits = jax.random.split(jax.random.key(seed), 8)
    return {
        "activations": normal_values(splits[0], (TOKENS, D), 1.0, 6.0, ((0, 16), (1, 16))),
        "grad_output": normal_values(splits[1], (TOKENS, D), 1.0, 6.0, ((0, 16), (1, 16))),
        "gate_pre": normal_values(splits[2], (TOKENS, FF), 1.5, 8.0, ((0, 16), (1, 16))),
        "up_pre": normal_values(splits[3], (TOKENS, FF), 1.0, 6.0, ((0, 16), (1, 16))),
        "w_gate": normal_values(splits[4], (D, FF), D ** -0.5, 0.046875, ((0, 16), (1, 16))),
        "w_up": normal_values(splits[5], (D, FF), D ** -0.5, 0.046875, ((0, 16), (1, 16))),
        "w_down": normal_values(splits[6], (FF, D), FF ** -0.5, 0.0625, ((0, 16), (1, 16))),
    }


def reference(activations, grad_output, gate_pre, up_pre, w_gate, w_up, w_down):
    gate_val = gate_pre.astype(jnp.float32)
    up_val = up_pre.astype(jnp.float32)
    sigma = 1.0 / (1.0 + jnp.exp(-gate_val))
    hidden = (gate_val * sigma * up_val).astype(jnp.bfloat16)
    grad_hidden = lax.dot_general(grad_output, w_down, (((1,), (1,)), ((), ())), preferred_element_type=jnp.float32)
    grad_gate_pre = (grad_hidden * up_val * sigma * (1.0 + gate_val * (1.0 - sigma))).astype(jnp.bfloat16)
    grad_up_pre = (grad_hidden * gate_val * sigma).astype(jnp.bfloat16)
    contract_rows = (((0,), (0,)), ((), ()))
    grad_down = lax.dot_general(hidden, grad_output, contract_rows, preferred_element_type=jnp.float32).astype(jnp.bfloat16)
    grad_gate = lax.dot_general(activations, grad_gate_pre, contract_rows, preferred_element_type=jnp.float32).astype(jnp.bfloat16)
    grad_up = lax.dot_general(activations, grad_up_pre, contract_rows, preferred_element_type=jnp.float32).astype(jnp.bfloat16)
    contract_cols = (((1,), (1,)), ((), ()))
    grad_input = lax.dot_general(grad_gate_pre, w_gate, contract_cols, preferred_element_type=jnp.float32)
    grad_input = grad_input + lax.dot_general(grad_up_pre, w_up, contract_cols, preferred_element_type=jnp.float32)
    return grad_input.astype(jnp.bfloat16), grad_gate, grad_up, grad_down
```

```python
import jax
import jax.numpy as jnp
from jax import lax
from jax.experimental import pallas as pl
from jax.experimental.pallas import tpu as pltpu
from jax.sharding import Mesh, PartitionSpec as P

AXES = ("x", "y", "z", "core")
DIMS = (4, 4, 8, 2)
F32 = jnp.float32
BF16 = jnp.bfloat16


def device_pairs(target):
    def number(x, y, z, k):
        return ((x % 4 * 4 + y % 4) * 8 + z % 8) * 2 + k % 2

    return [
        (number(x, y, z, k), number(*target(x, y, z, k)))
        for x in range(4)
        for y in range(4)
        for z in range(8)
        for k in range(2)
    ]


def send(value, target):
    return lax.ppermute(value, AXES, device_pairs(target))


def round_z(value):
    return send(value, lambda x, y, z, k: (x, y, z + 1 - 2 * k, k))


def other_core(value):
    return send(value, lambda x, y, z, k: (x, y, z, k + 1))


def along_a(value, step):
    return send(
        value,
        lambda x, y, z, k: (x + step, y, z, k) if k == 0 else (x, y + step, z, k),
    )


def along_b(value, step):
    return send(
        value,
        lambda x, y, z, k: (x, y + step, z, k) if k == 0 else (x + step, y, z, k),
    )


def gather_rows(value):
    got = {0: value}
    for step in (2, 1, 3):
        got[(-step) % 4] = along_b(value, step)
    line = jnp.concatenate([got[i] for i in range(4)], axis=0)
    got = {0: line}
    for step in (2, 1, 3):
        got[(-step) % 4] = along_a(line, step)
    return [got[i] for i in range(4)]


def join(*values):
    return lax.optimization_barrier(values)


def pair_product(order, *refs):
    out = refs[-1]
    total = None
    for i in range(0, len(refs) - 1, 3):
        first, second, weights = refs[i : i + 3]
        both = jnp.concatenate([first[...], second[...]], axis=0)
        part = lax.dot_general(
            both, weights[...], (((1,), (1,)), ((), ())), preferred_element_type=F32
        )
        total = part if total is None else total + part
    out[...] = total.astype(out.dtype)


def block_product(terms, order, dtype):
    n = order.shape[0]
    rows = terms[0][0].shape[0] // 16
    width, depth = terms[0][1].shape
    specs, operands = [], []
    for value, weights in terms:
        specs += [
            pl.BlockSpec((rows, depth), lambda i, at: (at[2 * i], 0)),
            pl.BlockSpec((rows, depth), lambda i, at: (at[2 * i + 1], 0)),
            pl.BlockSpec((width, depth), lambda i, at: (0, 0)),
        ]
        operands += [value, value, weights]
    grid_spec = pltpu.PrefetchScalarGridSpec(
        num_scalar_prefetch=1,
        grid=(n // 2,),
        in_specs=specs,
        out_specs=pl.BlockSpec((2 * rows, width), lambda i, at: (i, 0)),
    )
    return pl.pallas_call(
        pair_product,
        grid_spec=grid_spec,
        out_shape=jax.ShapeDtypeStruct((n * rows, width), dtype),
        compiler_params=pltpu.CompilerParams(vmem_limit_bytes=32 * 1024 * 1024),
        cost_estimate=pl.CostEstimate(
            flops=2 * len(terms) * n * rows * width * depth,
            bytes_accessed=2 * len(terms) * (n * rows + width) * depth
            + n * rows * width * jnp.dtype(dtype).itemsize,
            transcendentals=0,
        ),
    )(order, *operands)


def swiglu_hidden(order, pre_ref, *refs):
    out = refs[-1]
    ff = out.shape[1]
    gate_val = pre_ref[:, :ff].astype(F32)
    up_val = pre_ref[:, ff:].astype(F32)
    sigma = 1.0 / (1.0 + jnp.exp(-gate_val))
    out[...] = (gate_val * sigma * up_val).astype(BF16)


def swiglu_grads(order, pre_ref, hidden_ref, *refs):
    gate_out, up_out = refs[-2:]
    ff = gate_out.shape[1]
    grad = hidden_ref[...].astype(F32)
    gate_val = pre_ref[:, :ff].astype(F32)
    up_val = pre_ref[:, ff:].astype(F32)
    sigma = 1.0 / (1.0 + jnp.exp(-gate_val))
    gate_out[...] = (
        grad * up_val * sigma * (1.0 + gate_val * (1.0 - sigma))
    ).astype(BF16)
    up_out[...] = (grad * gate_val * sigma).astype(BF16)


def in_token_order(body, count, order, pieces):
    rows, width = pieces[0][0].shape[0] // 4, pieces[0][0].shape[1] // 2
    shape = jax.ShapeDtypeStruct((16 * rows, width), BF16)
    outs = ()
    for i in (0, 2, 3, 1):
        piece = pieces[i]
        outs = pl.pallas_call(
            body,
            grid_spec=pltpu.PrefetchScalarGridSpec(
                num_scalar_prefetch=1,
                grid=(4,),
                in_specs=[
                    pl.BlockSpec((rows, value.shape[1]), lambda j, at: (j, 0))
                    for value in piece
                ]
                + [pl.BlockSpec(memory_space=pl.ANY)] * len(outs),
                out_specs=[
                    pl.BlockSpec((rows, width), lambda j, at, i=i: (at[4 * i + j], 0))
                ]
                * count,
            ),
            out_shape=[shape] * count,
            input_output_aliases=(
                {1 + len(piece) + j: j for j in range(count)} if outs else {}
            ),
            compiler_params=pltpu.CompilerParams(vmem_limit_bytes=32 * 1024 * 1024),
            cost_estimate=pl.CostEstimate(
                flops=48 * rows * width,
                bytes_accessed=40 * rows * width,
                transcendentals=8 * rows * width,
            ),
        )(order, *piece, *outs)
    return outs


def local(activations, grad_output, gate_pre, up_pre, w_gate, w_up, w_down):
    contract_rows = (((0,), (0,)), ((), ()))
    x, y, z, k = [lax.axis_index(name) for name in AXES]
    a0 = jnp.where(k == 0, x, y)
    b0 = jnp.where(k == 0, y, x)
    ff = gate_pre.shape[1]
    rows = gate_pre.shape[0]
    way = 1 - 2 * k

    def block_at(position):
        a = (a0 + position // 4) % 4
        b = (b0 + position % 4) % 4
        return jnp.where(k == 0, 4 * a + b, 4 * b + a)

    def blocks(steps, swapped):
        steps, swapped = jnp.array(steps), jnp.array(swapped)
        return 2 * ((z + steps * way + 8) % 8) + (k + swapped) % 2

    order = block_at(jnp.arange(16, dtype=jnp.int32))
    send_far = blocks((4, 0, -3, -3), (1, 1, 1, 0))
    keep_far = blocks((4, 0, 3, 3), (0, 0, 0, 1))
    send_near = blocks((-2, -2, -1, -1), (1, 0, 1, 0))
    keep_near = blocks((2, 2, 1, 1), (0, 1, 0, 1))

    grad_whole = lax.all_gather(grad_output, ("z", "core"), axis=0, tiled=True)

    pre = gather_rows(jnp.concatenate([gate_pre, up_pre], axis=1))
    (hidden,) = in_token_order(swiglu_hidden, 1, order, [(v,) for v in pre])
    hidden, acts, grad_whole = join(hidden, activations, grad_whole)
    acts_whole = lax.all_gather(acts, ("z", "core"), axis=0, tiled=True)

    shares = {}
    for step in (2, 1, 3):
        share = block_product(
            [(grad_whole, w_down)], order[4 * step : 4 * step + 4], BF16
        )
        shares[step] = along_a(share, step)
    total = block_product([(grad_whole, w_down)], order[:4], F32)
    grad_down = lax.dot_general(
        hidden, grad_whole, contract_rows, preferred_element_type=F32
    ).astype(BF16)
    grad_down, total, *got = join(grad_down, total, *shares.values())
    for share in got:
        total = total + share.astype(F32)
    grad_hidden = total[:rows]
    for step in (2, 1, 3):
        share = total[step * rows : (step + 1) * rows]
        grad_hidden = grad_hidden + along_b(share, step)
    grad_hidden = gather_rows(grad_hidden.astype(BF16))
    grad_gate_pre, grad_up_pre = in_token_order(
        swiglu_grads, 2, order, list(zip(pre, grad_hidden))
    )

    terms = [(grad_gate_pre, w_gate), (grad_up_pre, w_up)]
    far = other_core(block_product(terms, send_far, F32))
    far = block_product(terms, keep_far, F32) + far
    near = other_core(block_product(terms, send_near, F32))
    near = block_product(terms, keep_near, F32) + near
    got = round_z(far[:rows].astype(BF16))
    got, near, acts_whole = join(got, near, acts_whole)
    mine = jnp.concatenate(
        [far[2 * rows : 3 * rows] + got.astype(F32), far[3 * rows :]], axis=0
    )
    got = round_z(mine.astype(BF16))
    grad_gate = lax.dot_general(
        acts_whole, grad_gate_pre, contract_rows, preferred_element_type=F32
    ).astype(BF16)
    got, grad_gate = join(got, grad_gate)
    mine = near[: 2 * rows] + got.astype(F32)
    got = round_z(mine.astype(BF16))
    grad_up = lax.dot_general(
        acts_whole, grad_up_pre, contract_rows, preferred_element_type=F32
    ).astype(BF16)
    got, grad_up = join(got, grad_up)
    mine = near[2 * rows :] + got.astype(F32)
    got = round_z(mine.astype(BF16)).astype(F32)
    grad_input = far[rows : 2 * rows] + got[:rows] + other_core(got[rows:])
    return (grad_input.astype(BF16), grad_gate, grad_up, grad_down)


def solution(mesh):
    grid = Mesh(mesh.devices.reshape(DIMS), AXES)
    row, col = ("x", "y"), ("z", "core")
    in_specs = (
        P(col, row),
        P(col, row),
        P(row, col),
        P(row, col),
        P(row, col),
        P(row, col),
        P(col, row),
    )
    out_specs = (P(col, row), P(row, col), P(row, col), P(col, row))
    return jax.shard_map(
        local, mesh=grid, in_specs=in_specs, out_specs=out_specs, check_vma=False
    )
```

```python
import jax
import jax.numpy as jnp
from jax import lax
from jax.experimental import pallas as pl
from jax.experimental.pallas import tpu as pltpu
from jax.sharding import Mesh, PartitionSpec as P

AXES = ("x", "y", "z", "core")
DIMS = (4, 4, 8, 2)
F32 = jnp.float32
BF16 = jnp.bfloat16
LIGHT = pl.CostEstimate(flops=1024, bytes_accessed=1024, transcendentals=0)


def device_pairs(target):
    def number(x, y, z, k):
        return ((x % 4 * 4 + y % 4) * 8 + z % 8) * 2 + k % 2

    return [
        (number(x, y, z, k), number(*target(x, y, z, k)))
        for x in range(4)
        for y in range(4)
        for z in range(8)
        for k in range(2)
    ]


def send(value, target):
    return lax.ppermute(value, AXES, device_pairs(target))


def round_z(value):
    return send(value, lambda x, y, z, k: (x, y, z + 1 - 2 * k, k))


def other_core(value):
    return send(value, lambda x, y, z, k: (x, y, z, k + 1))


def along_a(value, step):
    return send(
        value,
        lambda x, y, z, k: (x + step, y, z, k) if k == 0 else (x, y + step, z, k),
    )


def along_b(value, step):
    return send(
        value,
        lambda x, y, z, k: (x, y + step, z, k) if k == 0 else (x + step, y, z, k),
    )


def gather_rows(value):
    got = {0: value}
    for step in (2, 1, 3):
        got[(-step) % 4] = along_b(value, step)
    line = jnp.concatenate([got[i] for i in range(4)], axis=0)
    got = {0: line}
    for step in (2, 1, 3):
        got[(-step) % 4] = along_a(line, step)
    return [got[i] for i in range(4)]


def join(*values):
    return lax.optimization_barrier(values)


def pair_product(order, *refs):
    out = refs[-1]
    total = None
    for i in range(0, len(refs) - 1, 3):
        first, second, weights = refs[i : i + 3]
        both = jnp.concatenate([first[...], second[...]], axis=0)
        part = lax.dot_general(
            both, weights[...], (((1,), (1,)), ((), ())), preferred_element_type=F32
        )
        total = part if total is None else total + part
    out[...] = total.astype(out.dtype)


def block_product(terms, order, dtype, cost=None):
    n = order.shape[0]
    rows = terms[0][0].shape[0] // 16
    width, depth = terms[0][1].shape
    specs, operands = [], []
    for value, weights in terms:
        specs += [
            pl.BlockSpec((rows, depth), lambda i, at: (at[2 * i], 0)),
            pl.BlockSpec((rows, depth), lambda i, at: (at[2 * i + 1], 0)),
            pl.BlockSpec((width, depth), lambda i, at: (0, 0)),
        ]
        operands += [value, value, weights]
    grid_spec = pltpu.PrefetchScalarGridSpec(
        num_scalar_prefetch=1,
        grid=(n // 2,),
        in_specs=specs,
        out_specs=pl.BlockSpec((2 * rows, width), lambda i, at: (i, 0)),
    )
    return pl.pallas_call(
        pair_product,
        grid_spec=grid_spec,
        out_shape=jax.ShapeDtypeStruct((n * rows, width), dtype),
        compiler_params=pltpu.CompilerParams(vmem_limit_bytes=32 * 1024 * 1024),
        cost_estimate=cost
        or pl.CostEstimate(
            flops=2 * len(terms) * n * rows * width * depth,
            bytes_accessed=2 * len(terms) * (n * rows + width) * depth
            + n * rows * width * jnp.dtype(dtype).itemsize,
            transcendentals=0,
        ),
    )(order, *operands)


def swiglu_hidden(order, pre_ref, *refs):
    out = refs[-1]
    ff = out.shape[1]
    gate_val = pre_ref[:, :ff].astype(F32)
    up_val = pre_ref[:, ff:].astype(F32)
    sigma = 1.0 / (1.0 + jnp.exp(-gate_val))
    out[...] = (gate_val * sigma * up_val).astype(BF16)


def in_token_order(body, count, order, pieces):
    rows, width = pieces[0][0].shape[0] // 4, pieces[0][0].shape[1] // 2
    shape = jax.ShapeDtypeStruct((16 * rows, width), BF16)
    outs = ()
    for i in (0, 2, 3, 1):
        piece = pieces[i]
        outs = pl.pallas_call(
            body,
            grid_spec=pltpu.PrefetchScalarGridSpec(
                num_scalar_prefetch=1,
                grid=(4,),
                in_specs=[
                    pl.BlockSpec((rows, value.shape[1]), lambda j, at: (j, 0))
                    for value in piece
                ]
                + [pl.BlockSpec(memory_space=pl.ANY)] * len(outs),
                out_specs=[
                    pl.BlockSpec((rows, width), lambda j, at, i=i: (at[4 * i + j], 0))
                ]
                * count,
            ),
            out_shape=[shape] * count,
            input_output_aliases=(
                {1 + len(piece) + j: j for j in range(count)} if outs else {}
            ),
            compiler_params=pltpu.CompilerParams(vmem_limit_bytes=32 * 1024 * 1024),
            cost_estimate=pl.CostEstimate(
                flops=48 * rows * width,
                bytes_accessed=40 * rows * width,
                transcendentals=8 * rows * width,
            ),
        )(order, *piece, *outs)
    return outs


def swiglu_piece(hidden_ref, pre_ref, *refs):
    gate_out, up_out = refs[-2:]
    ff = gate_out.shape[1]
    grad = hidden_ref[...].astype(F32)
    gate_val = pre_ref[:, :ff].astype(F32)
    up_val = pre_ref[:, ff:].astype(F32)
    sigma = 1.0 / (1.0 + jnp.exp(-gate_val))
    gate_out[...] = (
        grad * up_val * sigma * (1.0 + gate_val * (1.0 - sigma))
    ).astype(BF16)
    up_out[...] = (grad * gate_val * sigma).astype(BF16)


def swiglu_grads(grad_hidden, pre):
    rows, ff = grad_hidden[0].shape
    part = rows // 2
    shape = jax.ShapeDtypeStruct((4 * rows, ff), BF16)
    outs = ()
    for i in (0, 2, 3, 1):
        outs = pl.pallas_call(
            swiglu_piece,
            grid=(2,),
            in_specs=[
                pl.BlockSpec((part, ff), lambda j: (j, 0)),
                pl.BlockSpec((part, 2 * ff), lambda j: (j, 0)),
            ]
            + [pl.BlockSpec(memory_space=pl.ANY)] * len(outs),
            out_specs=[
                pl.BlockSpec((part, ff), lambda j, i=i: (2 * i + j, 0)),
                pl.BlockSpec((part, ff), lambda j, i=i: (2 * i + j, 0)),
            ],
            out_shape=[shape, shape],
            input_output_aliases={2: 0, 3: 1} if outs else {},
            compiler_params=pltpu.CompilerParams(vmem_limit_bytes=32 * 1024 * 1024),
            cost_estimate=pl.CostEstimate(
                flops=12 * rows * ff,
                bytes_accessed=10 * rows * ff,
                transcendentals=2 * rows * ff,
            ),
        )(grad_hidden[i], pre[i], *outs)
    return outs


def copy_blocks(order, *refs):
    refs[-1][...] = jnp.concatenate([ref[...] for ref in refs[:-1]], axis=0)


def reorder(value, order):
    rows, width = value.shape[0] // 16, value.shape[1]
    return pl.pallas_call(
        copy_blocks,
        grid_spec=pltpu.PrefetchScalarGridSpec(
            num_scalar_prefetch=1,
            grid=(4,),
            in_specs=[
                pl.BlockSpec((rows, width), lambda i, at, j=j: (at[4 * i + j], 0))
                for j in range(4)
            ],
            out_specs=pl.BlockSpec((4 * rows, width), lambda i, at: (i, 0)),
        ),
        out_shape=jax.ShapeDtypeStruct(value.shape, value.dtype),
        compiler_params=pltpu.CompilerParams(vmem_limit_bytes=32 * 1024 * 1024),
        cost_estimate=LIGHT,
    )(order, value, value, value, value)


def local(activations, grad_output, gate_pre, up_pre, w_gate, w_up, w_down):
    contract_rows = (((0,), (0,)), ((), ()))
    x, y, z, k = [lax.axis_index(name) for name in AXES]
    a0 = jnp.where(k == 0, x, y)
    b0 = jnp.where(k == 0, y, x)
    ff = gate_pre.shape[1]
    rows = gate_pre.shape[0]
    way = 1 - 2 * k

    def place(block):
        up, along = block // 4, block % 4
        a = jnp.where(k == 0, up, along)
        b = jnp.where(k == 0, along, up)
        return (a - a0) % 4 * 4 + (b - b0) % 4

    def block_at(position):
        a = (a0 + position // 4) % 4
        b = (b0 + position % 4) % 4
        return jnp.where(k == 0, 4 * a + b, 4 * b + a)

    def blocks(steps, swapped):
        steps, swapped = jnp.array(steps), jnp.array(swapped)
        return place(2 * ((z + steps * way + 8) % 8) + (k + swapped) % 2)

    order = block_at(jnp.arange(16, dtype=jnp.int32))
    send_far = blocks((4, 0, -3, -3), (1, 1, 1, 0))
    keep_far = blocks((4, 0, 3, 3), (0, 0, 0, 1))
    send_near = blocks((-2, -2, -1, -1), (1, 0, 1, 0))
    keep_near = blocks((2, 2, 1, 1), (0, 1, 0, 1))

    grad_whole = lax.all_gather(grad_output, ("z", "core"), axis=0, tiled=True)

    pre = gather_rows(jnp.concatenate([gate_pre, up_pre], axis=1))
    (hidden,) = in_token_order(swiglu_hidden, 1, order, [(v,) for v in pre])
    hidden, acts, grad_whole = join(hidden, activations, grad_whole)
    acts_whole = lax.all_gather(acts, ("z", "core"), axis=0, tiled=True)

    shares = {}
    for step in (2, 1, 3):
        share = block_product(
            [(grad_whole, w_down)], order[4 * step : 4 * step + 4], BF16
        )
        shares[step] = along_a(share, step)
    total = block_product([(grad_whole, w_down)], order[:4], F32)
    grad_down = lax.dot_general(
        hidden, grad_whole, contract_rows, preferred_element_type=F32
    ).astype(BF16)
    grad_down, total, *got = join(grad_down, total, *shares.values())
    for share in got:
        total = total + share.astype(F32)
    grad_hidden = total[:rows]
    for step in (2, 1, 3):
        share = total[step * rows : (step + 1) * rows]
        grad_hidden = grad_hidden + along_b(share, step)
    grad_hidden = gather_rows(grad_hidden.astype(BF16))
    grad_gate_pre, grad_up_pre = swiglu_grads(grad_hidden, pre)

    terms = [(grad_gate_pre, w_gate), (grad_up_pre, w_up)]
    far = other_core(block_product(terms, send_far, F32, LIGHT))
    keep = block_product(terms, keep_far, F32, LIGHT)
    first = (keep[:rows] + far[:rows]).astype(BF16)
    gate_term, up_term, first, keep, far = join(
        grad_gate_pre, grad_up_pre, first, keep, far
    )
    terms = [(gate_term, w_gate), (up_term, w_up)]
    got = round_z(first)
    near = other_core(block_product(terms, send_near, F32, LIGHT))
    near = block_product(terms, keep_near, F32, LIGHT) + near
    far = keep + far
    got, near, acts_whole = join(got, near, acts_whole)
    mine = jnp.concatenate(
        [far[2 * rows : 3 * rows] + got.astype(F32), far[3 * rows :]], axis=0
    )
    got = round_z(mine.astype(BF16))
    acts_whole = reorder(acts_whole, order)
    got, acts_whole = join(got, acts_whole)
    mine = near[: 2 * rows] + got.astype(F32)
    got = round_z(mine.astype(BF16))
    grad_gate = lax.dot_general(
        acts_whole, gate_term, contract_rows, preferred_element_type=F32
    ).astype(BF16)
    got, grad_gate = join(got, grad_gate)
    mine = near[2 * rows :] + got.astype(F32)
    got = round_z(mine.astype(BF16))
    grad_up = lax.dot_general(
        acts_whole, up_term, contract_rows, preferred_element_type=F32
    ).astype(BF16)
    got, grad_up = join(got, grad_up)
    got = got.astype(F32)
    grad_input = far[rows : 2 * rows] + got[:rows] + other_core(got[rows:])
    return (grad_input.astype(BF16), grad_gate, grad_up, grad_down)


def solution(mesh):
    grid = Mesh(mesh.devices.reshape(DIMS), AXES)
    row, col = ("x", "y"), ("z", "core")
    in_specs = (
        P(col, row),
        P(col, row),
        P(row, col),
        P(row, col),
        P(row, col),
        P(row, col),
        P(col, row),
    )
    out_specs = (P(col, row), P(row, col), P(row, col), P(col, row))
    return jax.shard_map(
        local, mesh=grid, in_specs=in_specs, out_specs=out_specs, check_vma=False
    )
```

```python
import jax
import jax.numpy as jnp
from jax import lax
from jax.experimental import pallas as pl
from jax.experimental.pallas import tpu as pltpu
from jax.sharding import Mesh, PartitionSpec as P

AXES = ("x", "y", "z", "core")
DIMS = (4, 4, 8, 2)
F32 = jnp.float32
BF16 = jnp.bfloat16
LIGHT = pl.CostEstimate(flops=1024, bytes_accessed=1024, transcendentals=0)


def device_pairs(target):
    def number(x, y, z, k):
        return ((x % 4 * 4 + y % 4) * 8 + z % 8) * 2 + k % 2

    return [
        (number(x, y, z, k), number(*target(x, y, z, k)))
        for x in range(4)
        for y in range(4)
        for z in range(8)
        for k in range(2)
    ]


def send(value, target):
    return lax.ppermute(value, AXES, device_pairs(target))


def round_z(value):
    return send(value, lambda x, y, z, k: (x, y, z + 1 - 2 * k, k))


def other_core(value):
    return send(value, lambda x, y, z, k: (x, y, z, k + 1))


def along_a(value, step):
    return send(
        value,
        lambda x, y, z, k: (x + step, y, z, k) if k == 0 else (x, y + step, z, k),
    )


def along_b(value, step):
    return send(
        value,
        lambda x, y, z, k: (x, y + step, z, k) if k == 0 else (x + step, y, z, k),
    )


def gather_rows(value):
    got = {0: value}
    for step in (2, 1, 3):
        got[(-step) % 4] = along_b(value, step)
    line = jnp.concatenate([got[i] for i in range(4)], axis=0)
    got = {0: line}
    for step in (2, 1, 3):
        got[(-step) % 4] = along_a(line, step)
    return [got[i] for i in range(4)]


def join(*values):
    return lax.optimization_barrier(values)


def pair_product(order, *refs):
    out = refs[-1]
    total = None
    for i in range(0, len(refs) - 1, 3):
        first, second, weights = refs[i : i + 3]
        both = jnp.concatenate([first[...], second[...]], axis=0)
        part = lax.dot_general(
            both, weights[...], (((1,), (1,)), ((), ())), preferred_element_type=F32
        )
        total = part if total is None else total + part
    out[...] = total.astype(out.dtype)


def block_product(terms, order, dtype, cost=None):
    n = order.shape[0]
    rows = terms[0][0].shape[0] // 16
    width, depth = terms[0][1].shape
    specs, operands = [], []
    for value, weights in terms:
        specs += [
            pl.BlockSpec((rows, depth), lambda i, at: (at[2 * i], 0)),
            pl.BlockSpec((rows, depth), lambda i, at: (at[2 * i + 1], 0)),
            pl.BlockSpec((width, depth), lambda i, at: (0, 0)),
        ]
        operands += [value, value, weights]
    grid_spec = pltpu.PrefetchScalarGridSpec(
        num_scalar_prefetch=1,
        grid=(n // 2,),
        in_specs=specs,
        out_specs=pl.BlockSpec((2 * rows, width), lambda i, at: (i, 0)),
    )
    return pl.pallas_call(
        pair_product,
        grid_spec=grid_spec,
        out_shape=jax.ShapeDtypeStruct((n * rows, width), dtype),
        compiler_params=pltpu.CompilerParams(vmem_limit_bytes=32 * 1024 * 1024),
        cost_estimate=cost
        or pl.CostEstimate(
            flops=2 * len(terms) * n * rows * width * depth,
            bytes_accessed=2 * len(terms) * (n * rows + width) * depth
            + n * rows * width * jnp.dtype(dtype).itemsize,
            transcendentals=0,
        ),
    )(order, *operands)


def swiglu_hidden(order, pre_ref, *refs):
    out = refs[-1]
    ff = out.shape[1]
    gate_val = pre_ref[:, :ff].astype(F32)
    up_val = pre_ref[:, ff:].astype(F32)
    sigma = 1.0 / (1.0 + jnp.exp(-gate_val))
    out[...] = (gate_val * sigma * up_val).astype(BF16)


def in_token_order(body, count, order, pieces):
    rows, width = pieces[0][0].shape[0] // 4, pieces[0][0].shape[1] // 2
    shape = jax.ShapeDtypeStruct((16 * rows, width), BF16)
    outs = ()
    for i in (0, 2, 3, 1):
        piece = pieces[i]
        outs = pl.pallas_call(
            body,
            grid_spec=pltpu.PrefetchScalarGridSpec(
                num_scalar_prefetch=1,
                grid=(4,),
                in_specs=[
                    pl.BlockSpec((rows, value.shape[1]), lambda j, at: (j, 0))
                    for value in piece
                ]
                + [pl.BlockSpec(memory_space=pl.ANY)] * len(outs),
                out_specs=[
                    pl.BlockSpec((rows, width), lambda j, at, i=i: (at[4 * i + j], 0))
                ]
                * count,
            ),
            out_shape=[shape] * count,
            input_output_aliases=(
                {1 + len(piece) + j: j for j in range(count)} if outs else {}
            ),
            compiler_params=pltpu.CompilerParams(vmem_limit_bytes=32 * 1024 * 1024),
            cost_estimate=pl.CostEstimate(
                flops=48 * rows * width,
                bytes_accessed=40 * rows * width,
                transcendentals=8 * rows * width,
            ),
        )(order, *piece, *outs)
    return outs


def swiglu_piece(hidden_ref, pre_ref, *refs):
    gate_out, up_out = refs[-2:]
    ff = gate_out.shape[1]
    grad = hidden_ref[...].astype(F32)
    gate_val = pre_ref[:, :ff].astype(F32)
    up_val = pre_ref[:, ff:].astype(F32)
    sigma = 1.0 / (1.0 + jnp.exp(-gate_val))
    gate_out[...] = (
        grad * up_val * sigma * (1.0 + gate_val * (1.0 - sigma))
    ).astype(BF16)
    up_out[...] = (grad * gate_val * sigma).astype(BF16)


def swiglu_grads(grad_hidden, pre):
    rows, ff = grad_hidden[0].shape
    part = rows // 2
    shape = jax.ShapeDtypeStruct((4 * rows, ff), BF16)
    outs = ()
    for i in (0, 2, 3, 1):
        outs = pl.pallas_call(
            swiglu_piece,
            grid=(2,),
            in_specs=[
                pl.BlockSpec((part, ff), lambda j: (j, 0)),
                pl.BlockSpec((part, 2 * ff), lambda j: (j, 0)),
            ]
            + [pl.BlockSpec(memory_space=pl.ANY)] * len(outs),
            out_specs=[
                pl.BlockSpec((part, ff), lambda j, i=i: (2 * i + j, 0)),
                pl.BlockSpec((part, ff), lambda j, i=i: (2 * i + j, 0)),
            ],
            out_shape=[shape, shape],
            input_output_aliases={2: 0, 3: 1} if outs else {},
            compiler_params=pltpu.CompilerParams(vmem_limit_bytes=32 * 1024 * 1024),
            cost_estimate=pl.CostEstimate(
                flops=12 * rows * ff,
                bytes_accessed=10 * rows * ff,
                transcendentals=2 * rows * ff,
            ),
        )(grad_hidden[i], pre[i], *outs)
    return outs


def copy_blocks(order, *refs):
    refs[-1][...] = jnp.concatenate([ref[...] for ref in refs[:-1]], axis=0)


def reorder(value, order):
    rows, width = value.shape[0] // 16, value.shape[1]
    return pl.pallas_call(
        copy_blocks,
        grid_spec=pltpu.PrefetchScalarGridSpec(
            num_scalar_prefetch=1,
            grid=(4,),
            in_specs=[
                pl.BlockSpec((rows, width), lambda i, at, j=j: (at[4 * i + j], 0))
                for j in range(4)
            ],
            out_specs=pl.BlockSpec((4 * rows, width), lambda i, at: (i, 0)),
        ),
        out_shape=jax.ShapeDtypeStruct(value.shape, value.dtype),
        compiler_params=pltpu.CompilerParams(vmem_limit_bytes=32 * 1024 * 1024),
        cost_estimate=LIGHT,
    )(order, value, value, value, value)


def local(activations, grad_output, gate_pre, up_pre, w_gate, w_up, w_down):
    contract_rows = (((0,), (0,)), ((), ()))
    x, y, z, k = [lax.axis_index(name) for name in AXES]
    a0 = jnp.where(k == 0, x, y)
    b0 = jnp.where(k == 0, y, x)
    ff = gate_pre.shape[1]
    rows = gate_pre.shape[0]
    way = 1 - 2 * k

    def place(block):
        up, along = block // 4, block % 4
        a = jnp.where(k == 0, up, along)
        b = jnp.where(k == 0, along, up)
        return (a - a0) % 4 * 4 + (b - b0) % 4

    def block_at(position):
        a = (a0 + position // 4) % 4
        b = (b0 + position % 4) % 4
        return jnp.where(k == 0, 4 * a + b, 4 * b + a)

    def blocks(steps, swapped):
        steps, swapped = jnp.array(steps), jnp.array(swapped)
        return place(2 * ((z + steps * way + 8) % 8) + (k + swapped) % 2)

    order = block_at(jnp.arange(16, dtype=jnp.int32))
    send_far = blocks((4, 0, -3, -3), (1, 1, 1, 0))
    keep_far = blocks((4, 0, 3, 3), (0, 0, 0, 1))
    send_near = blocks((-2, -2, -1, -1), (1, 0, 1, 0))
    keep_near = blocks((2, 2, 1, 1), (0, 1, 0, 1))

    grad_whole = lax.all_gather(grad_output, ("z", "core"), axis=0, tiled=True)

    pre = gather_rows(jnp.concatenate([gate_pre, up_pre], axis=1))
    (hidden,) = in_token_order(swiglu_hidden, 1, order, [(v,) for v in pre])
    hidden, acts, grad_whole = join(hidden, activations, grad_whole)
    acts_whole = lax.all_gather(acts, ("z", "core"), axis=0, tiled=True)

    shares = {}
    for step in (2, 1, 3):
        share = block_product(
            [(grad_whole, w_down)], order[4 * step : 4 * step + 4], BF16
        )
        shares[step] = along_a(share, step)
    total = block_product([(grad_whole, w_down)], order[:4], F32)
    grad_down = lax.dot_general(
        hidden, grad_whole, contract_rows, preferred_element_type=F32
    ).astype(BF16)
    grad_down, total, *got = join(grad_down, total, *shares.values())
    for share in got:
        total = total + share.astype(F32)
    grad_hidden = total[:rows]
    for step in (2, 1, 3):
        share = total[step * rows : (step + 1) * rows]
        grad_hidden = grad_hidden + along_b(share, step)
    grad_hidden = gather_rows(grad_hidden.astype(BF16))
    grad_gate_pre, grad_up_pre = swiglu_grads(grad_hidden, pre)

    terms = [(grad_gate_pre, w_gate), (grad_up_pre, w_up)]
    far = other_core(block_product(terms, send_far, F32, LIGHT))
    keep = block_product(terms, keep_far, F32, LIGHT)
    near = block_product(terms, send_near, F32, LIGHT)
    far, keep, near = join(far, keep, near)
    first = (keep[:rows] + far[:rows]).astype(BF16)
    gate_term, up_term, first, keep, far = join(
        grad_gate_pre, grad_up_pre, first, keep, far
    )
    terms = [(gate_term, w_gate), (up_term, w_up)]
    got = round_z(first)
    near = block_product(terms, keep_near, F32, LIGHT) + other_core(near)
    far = keep + far
    got, near, acts_whole = join(got, near, acts_whole)
    mine = jnp.concatenate(
        [far[2 * rows : 3 * rows] + got.astype(F32), far[3 * rows :]], axis=0
    )
    got = round_z(mine.astype(BF16))
    acts_whole = reorder(acts_whole, order)
    got, acts_whole = join(got, acts_whole)
    mine = near[: 2 * rows] + got.astype(F32)
    got = round_z(mine.astype(BF16))
    grad_gate = lax.dot_general(
        acts_whole, gate_term, contract_rows, preferred_element_type=F32
    ).astype(BF16)
    got, grad_gate = join(got, grad_gate)
    mine = near[2 * rows :] + got.astype(F32)
    got = round_z(mine.astype(BF16))
    grad_up = lax.dot_general(
        acts_whole, up_term, contract_rows, preferred_element_type=F32
    ).astype(BF16)
    got, grad_up = join(got, grad_up)
    got = got.astype(F32)
    grad_input = far[rows : 2 * rows] + got[:rows] + other_core(got[rows:])
    return (grad_input.astype(BF16), grad_gate, grad_up, grad_down)


def solution(mesh):
    grid = Mesh(mesh.devices.reshape(DIMS), AXES)
    row, col = ("x", "y"), ("z", "core")
    in_specs = (
        P(col, row),
        P(col, row),
        P(row, col),
        P(row, col),
        P(row, col),
        P(row, col),
        P(col, row),
    )
    out_specs = (P(col, row), P(row, col), P(row, col), P(col, row))
    return jax.shard_map(
        local, mesh=grid, in_specs=in_specs, out_specs=out_specs, check_vma=False
    )
```
